32 devices in a mesh: grp: 2 (over y), seq: 16 (over z, x, core).
Axes of the slice: x: 2, y: 2, z: 4, core: 2. Of those that a mesh axis runs over, the one named last changes fastest.
Arguments:
- queries: bfloat16 [8192, 1536], P(('grp', 'seq')), parts along dimension 0, may hold values from -6 to 6
- video_keys: bfloat16 [8192, 1536], P(('grp', 'seq')), parts along dimension 0, may hold values from -6 to 6
- video_values: bfloat16 [8192, 1536], P(('grp', 'seq')), parts along dimension 0, may hold values from -6 to 6
- attn_out: bfloat16 [8192, 1536], P(('grp', 'seq')), parts along dimension 0, may hold values from -1.796875 to 1.796875
- out_grad: bfloat16 [8192, 1536], P(('grp', 'seq')), parts along dimension 0, may hold values from -192 to 192
- log_sums: float32 [12, 8192], P(None, ('grp', 'seq')), parts along dimension 1, may hold values from 6.5 to 8
- text_keys: bfloat16 [512, 1536], P(('grp', 'seq')), parts along dimension 0, may hold values from -6 to 6
- text_values: bfloat16 [512, 1536], P(('grp', 'seq')), parts along dimension 0, may hold values from -6 to 6
- window: int32 [16, 3], replicated, may hold values from 0 to 1, as said below
- text_len: int32 [2], P('grp'), parts along dimension 0, may hold values from 64 to 256
Outputs:
- query_grad: bfloat16 [8192, 1536], P(('grp', 'seq')), parts along dimension 0
- key_grad: bfloat16 [8192, 1536], P(('grp', 'seq')), parts along dimension 0
- value_grad: bfloat16 [8192, 1536], P(('grp', 'seq')), parts along dimension 0
- textkey_grad: bfloat16 [512, 1536], P(('grp', 'seq')), parts along dimension 0
- textval_grad: bfloat16 [512, 1536], P(('grp', 'seq')), parts along dimension 0
The draws below stay inside these ranges and needn't reach their ends.
There are 2 independent parts, one for each index of `grp`. The reference program is written for one: setup_inputs(seed, part) draws one part's arguments, and reference() takes and returns one part's arrays. A program takes and returns all parts, laid end to end along the dimension named above; an argument that names none is the same for every part. Nothing has to cross between parts.
Inputs may be any that keep to these rules, and one draw needn't show every extreme that they name: window[t, o] is 1 where query tile t attends video tile t + o - 1, else 0; the middle entry o = 1 is always 1, and entries naming a tile outside 0 .. 15 are 0. Text tokens at positions text_len[0] and beyond are padding.
All inputs are finite; a program needn't handle non-finite values.
Results may differ from the reference program's by a relative error of at most 0.0057.
Values may be sent and summed in bfloat16 or wider, within the bound.
A program may use at most 64 MiB of HBM per device.

```python
import jax
import jax.numpy as jnp
from jax import lax

TILE = 256
HEADS = 12
HEAD_DIM = 128
TEXT = 256
REACH = 1
TILES = 16
TOKENS = 4096
WIDTH = 1536


def draw_window(key, part):
    key = jax.random.fold_in(key, 7)
    spread = 2 * REACH + 1
    picked = jax.random.randint(key, (TILES, spread), 0, 2)
    offsets = jnp.arange(spread)[None, :] - REACH
    target = jnp.arange(TILES)[:, None] + offsets
    inside = (target >= 0) & (target < TILES)
    picked = jnp.where(offsets == 0, 1, picked)
    return jnp.where(inside, picked, 0).astype(jnp.int32)


def level_of(own_key, extent, split, least, high):
    loudness, own = 1.0, jax.random.fold_in(own_key, 6)
    for dim, shards_of in split:
        steps = jnp.exp(jax.random.uniform(jax.random.fold_in(own, dim), (shards_of,), jnp.float32, least / len(split), high / len(split)))
        loudness = loudness * jnp.repeat(steps, extent[dim] // shards_of).reshape([-1 if axis == dim else 1 for axis in range(len(extent))])
    return loudness


def noise(own_key, shape, scale, limit, cuts=(), held_as=jnp.bfloat16):
    drawn = scale * jax.random.normal(own_key, shape, jnp.float32)
    if cuts:
        drawn = drawn * level_of(own_key, shape, cuts, -0.22, 0.18)
    return jnp.clip(drawn, -limit, limit).astype(held_as)


def setup_inputs(seed: int = 0, part: int = 0) -> dict:
    splits = jax.random.split(jax.random.key(seed), 11)
    part_splits = jax.random.split(jax.random.fold_in(splits[10], part), 11)
    queries = noise(part_splits[0], (TOKENS, WIDTH), 1.0, 6.0, ((0, 16),))
    video_keys = noise(part_splits[1], (TOKENS, WIDTH), 1.0, 6.0, ((0, 16),))
    video_values = noise(part_splits[2], (TOKENS, WIDTH), 1.0, 6.0, ((0, 16),))
    attn_out = noise(part_splits[3], (TOKENS, WIDTH), 0.3, 1.796875, ((0, 16),))
    out_grad = noise(part_splits[4], (TOKENS, WIDTH), 32.0, 192.0, ((0, 16),))
    log_sums = jnp.clip(6.5 + 1.5 * jax.random.uniform(part_splits[5], (HEADS, TOKENS), jnp.float32) ** level_of(part_splits[5], (HEADS, TOKENS), ((1, 16),), -0.2, 0.2), 6.5, 8.0)
    text_keys = noise(part_splits[6], (TEXT, WIDTH), 1.0, 6.0, ((0, 16),))
    text_values = noise(part_splits[7], (TEXT, WIDTH), 1.0, 6.0, ((0, 16),))
    window = draw_window(jax.random.fold_in(splits[10], 71), part)
    text_len = jax.random.randint(part_splits[9], (1,), TEXT // 4, TEXT + 1).astype(jnp.int32)
    return dict(queries=queries, video_keys=video_keys, video_values=video_values, attn_out=attn_out, out_grad=out_grad, log_sums=log_sums, text_keys=text_keys, text_values=text_values, window=window, text_len=text_len)


def rounded(value):
    return lax.optimization_barrier(value.astype(jnp.bfloat16)).astype(jnp.float32)


def block_grads(query_tile, grad_tile, sums_tile, deltas, key_tile, value_tile, column_w):
    factor = HEAD_DIM ** -0.5
    query_rows = query_tile.shape[0]
    key_rows = key_tile.shape[0]
    query_heads = query_tile.astype(jnp.float32).reshape(query_rows, HEADS, HEAD_DIM)
    grad_heads = grad_tile.astype(jnp.float32).reshape(query_rows, HEADS, HEAD_DIM)
    key_heads = key_tile.astype(jnp.float32).reshape(key_rows, HEADS, HEAD_DIM)
    value_heads = value_tile.astype(jnp.float32).reshape(key_rows, HEADS, HEAD_DIM)
    scores = jnp.einsum("qhd,khd->hqk", query_heads, key_heads) * factor
    probs = jnp.exp(scores - sums_tile[:, :, None]) * column_w[None, None, :]
    dprobs = jnp.einsum("qhd,khd->hqk", grad_heads, value_heads)
    dscores = rounded(probs * (dprobs - deltas[:, :, None]))
    probs_low = rounded(probs)
    query_term = jnp.einsum("hqk,khd->qhd", dscores, key_heads).reshape(query_rows, HEADS * HEAD_DIM) * factor
    key_term = jnp.einsum("hqk,qhd->khd", dscores, query_heads).reshape(key_rows, HEADS * HEAD_DIM) * factor
    value_term = jnp.einsum("hqk,qhd->khd", probs_low, grad_heads).reshape(key_rows, HEADS * HEAD_DIM)
    return query_term, key_term, value_term


def reference(queries, video_keys, video_values, attn_out, out_grad, log_sums, text_keys, text_values, window, text_len):
    features = HEADS * HEAD_DIM
    spread = 2 * REACH + 1
    deltas_all = jnp.sum((out_grad.astype(jnp.float32) * attn_out.astype(jnp.float32)).reshape(TOKENS, HEADS, HEAD_DIM), axis=2).T
    text_valid = (jnp.arange(TEXT) < text_len[0]).astype(jnp.float32)
    zero_block = jnp.zeros((TILE, features), jnp.float32)
    ones_cols = jnp.ones((TILE,), jnp.float32)

    def visit(loop_carry_state, tile_index):
        key_gradient_running, value_gradient_running, text_key_gradient_running, text_value_gradient_running = loop_carry_state
        row_start = (tile_index * TILE).astype(jnp.int32)
        query_tile = lax.dynamic_slice_in_dim(queries, row_start, TILE, 0)
        grad_tile = lax.dynamic_slice_in_dim(out_grad, row_start, TILE, 0)
        sums_tile = lax.dynamic_slice_in_dim(log_sums, row_start, TILE, 1)
        deltas = lax.dynamic_slice_in_dim(deltas_all, row_start, TILE, 1)
        text_q, text_k, caption_value_rows = block_grads(query_tile, grad_tile, sums_tile, deltas, text_keys, text_values, text_valid)
        query_gradient_running = rounded(text_q)
        text_key_gradient_running = text_key_gradient_running + text_k
        text_value_gradient_running = text_value_gradient_running + caption_value_rows
        window_row = lax.dynamic_slice_in_dim(window, tile_index.astype(jnp.int32), 1, 0)[0]
        for offset in range(spread):
            target = jnp.clip(tile_index + offset - REACH, 0, TILES - 1)
            key_start = (target * TILE).astype(jnp.int32)
            key_tile = lax.dynamic_slice_in_dim(video_keys, key_start, TILE, 0)
            value_tile = lax.dynamic_slice_in_dim(video_values, key_start, TILE, 0)

            def active():
                terms = block_grads(query_tile, grad_tile, sums_tile, deltas, key_tile, value_tile, ones_cols)
                return rounded(terms[0]), rounded(terms[1]), rounded(terms[2])

            def skipped():
                return zero_block, zero_block, zero_block

            grad_q, grad_k, grad_v = lax.cond(window_row[offset] > 0, active, skipped)
            query_gradient_running = query_gradient_running + grad_q
            old_keys = lax.dynamic_slice_in_dim(key_gradient_running, key_start, TILE, 0)
            key_gradient_running = lax.dynamic_update_slice_in_dim(key_gradient_running, old_keys + grad_k, key_start, 0)
            old_values = lax.dynamic_slice_in_dim(value_gradient_running, key_start, TILE, 0)
            value_gradient_running = lax.dynamic_update_slice_in_dim(value_gradient_running, old_values + grad_v, key_start, 0)
        return (key_gradient_running, value_gradient_running, text_key_gradient_running, text_value_gradient_running), query_gradient_running.astype(jnp.bfloat16)

    initial = (jnp.zeros((TOKENS, features), jnp.float32), jnp.zeros((TOKENS, features), jnp.float32),
               jnp.zeros((TEXT, features), jnp.float32), jnp.zeros((TEXT, features), jnp.float32))
    final_result, query_tiles = lax.scan(visit, initial, jnp.arange(TILES, dtype=jnp.int32))
    key_gradient_running, value_gradient_running, text_key_gradient_running, text_value_gradient_running = final_result
    query_grad = query_tiles.reshape(TOKENS, features)
    return (query_grad, key_gradient_running.astype(jnp.bfloat16), value_gradient_running.astype(jnp.bfloat16),
            text_key_gradient_running.astype(jnp.bfloat16), text_value_gradient_running.astype(jnp.bfloat16))
```

```python
import functools

import jax
import jax.numpy as jnp
from jax import lax
from jax.experimental import pallas as pl
from jax.experimental.pallas import tpu as pltpu
from jax.sharding import PartitionSpec as P

HEADS = 12
HEAD_DIM = 128
TEXT = 256
GROUP = 2
CHUNKS = HEADS // GROUP
FACTOR = HEAD_DIM ** (-0.5)
FAR = 1e30
MESH = pl.DeviceIdType.MESH


def mm(a, b, ca, cb):
    return lax.dot_general(a, b, (((ca,), (cb,)), ((), ())), preferred_element_type=jnp.float32)


def block_grads(q, g, k, v, sums, deltas, valid=None):
    probs = jnp.exp(mm(k, q, 1, 1) * FACTOR - sums)
    if valid is not None:
        probs = jnp.where(valid, probs, 0.0)
    dprobs = mm(v, g, 1, 1)
    dscores = (probs * (dprobs - deltas)).astype(jnp.bfloat16)
    dq = mm(dscores, k, 0, 0) * FACTOR
    dk = mm(dscores, q, 1, 0) * FACTOR
    dv = mm(probs.astype(jnp.bfloat16), g, 1, 0)
    return dq, dk, dv


def head(h):
    return pl.ds(pl.multiple_of(h * HEAD_DIM, HEAD_DIM), HEAD_DIM)


def kernel(
    n, inside, q_any, g_any, k_ref, v_ref, o_ref, sums_ref, tk_ref, tv_ref, win_ref, len_ref,
    dq_ref, dk_ref, dv_ref, tdk_ref, tdv_ref,
    q_ref, g_ref, nq, ng, stat, nstat, dq_sum, dk_sum, dv_sum, dq_out, dq_in, text, tgrad,
    local_sem, in_send, in_recv, stat_send, stat_recv, dq_send, dq_recv,
    *more,
):
    me = lax.axis_index("seq")
    has = (me > 0, me < n - 1)
    near = (me - 1, me + 1)
    share = TEXT // n
    half, outer = n // 2, n // 4
    core, cross_bit, layer = lax.rem(me, 2), lax.rem(me // 2, 2), me // 4
    mate, cross = me + 1 - 2 * core, me + 2 - 4 * cross_bit
    peers = [lax.rem(layer + d, outer) * 4 + lax.rem(me, 4) for d in range(1, outer)]

    loads = [
        pltpu.make_async_copy(q_any, q_ref, local_sem.at[0]),
        pltpu.make_async_copy(g_any, g_ref, local_sem.at[1]),
    ]
    for load in loads:
        load.start()

    def signal(device):
        pl.semaphore_signal(barrier, inc=1, device_id={"seq": device}, device_id_type=MESH)

    def remote(src, dst, send, recv, device):
        return pltpu.make_async_remote_copy(
            src_ref=src, dst_ref=dst, send_sem=send, recv_sem=recv,
            device_id={"seq": device}, device_id_type=MESH,
        )

    barrier = pltpu.get_barrier_semaphore()
    for side in range(2):
        pl.when(has[side])(functools.partial(signal, near[side]))
    far = [cross] + peers if inside else []
    for device in far:
        signal(device)
    pl.semaphore_wait(barrier, len(far) + sum(side.astype(jnp.int32) for side in has))

    def columns(c):
        return pl.ds(pl.multiple_of(c * GROUP * HEAD_DIM, GROUP * HEAD_DIM), GROUP * HEAD_DIM)

    def in_copies(side, c):
        there = 1 - side
        return [
            remote(
                src.at[:, columns(c)], dst.at[there, :, columns(c)],
                in_send.at[i, there, c], in_recv.at[i, there, c], near[side],
            )
            for i, (src, dst) in enumerate(((q_any, nq), (g_any, ng)))
        ]

    def stat_copy(side):
        there = 1 - side
        return remote(
            stat.at[side], nstat.at[there], stat_send.at[there], stat_recv.at[there], near[side]
        )

    def dq_copy(side, c):
        there = 1 - side
        return remote(
            dq_out.at[side, :, columns(c)], dq_in.at[there, :, columns(c)],
            dq_send.at[there, c], dq_recv.at[there, c], near[side],
        )

    if inside:
        t_send, t_recv, part1, got1, part2, got2, sum3, part3, got3, r1, r2, r3 = more

        def slot(device):
            return lax.rem(device, 2) * half + device // 2

        def rows(device):
            return pl.ds(pl.multiple_of(slot(device) * share, share), share)

        def text_copy(piece, device, index):
            ref = text.at[:, rows(piece), :]
            return remote(ref, ref, t_send.at[index], t_recv.at[piece], device)

        text[0, rows(me), :] = tk_ref[...]
        text[1, rows(me), :] = tv_ref[...]
        text_copies = []

        def push(piece, device):
            copy = text_copy(piece, device, len(text_copies))
            copy.start()
            text_copies.append(copy)

        push(me, cross)
        for peer in peers:
            push(me, peer)
        push(me, mate)

    for side in range(2):

        @pl.when(has[side])
        def _():
            def step(c, carry):
                for copy in in_copies(side, c):
                    copy.start()
                return carry

            lax.fori_loop(0, CHUNKS, step, 0)

    for load in loads:
        load.wait()

    def delta_step(h, carry):
        cols = head(h)
        prod = g_ref[:, cols].astype(jnp.float32) * o_ref[:, cols].astype(jnp.float32)
        row = jnp.sum(prod.T, axis=0, keepdims=True)
        for side in range(3):
            stat[side, pl.ds(HEADS + h, 1), :] = row
        return carry

    lax.fori_loop(0, HEADS, delta_step, 0)
    for index, offset in enumerate((0, 2, 1)):
        bias = jnp.where(win_ref[me, offset] > 0, 0.0, FAR).astype(jnp.float32)
        stat[index, :HEADS, :] = sums_ref[...] + bias
    for side in range(2):

        @pl.when(has[side])
        def _():
            stat_copy(side).start()

        @pl.when(jnp.logical_not(has[side]))
        def _():
            nq[side] = jnp.zeros(nq.shape[1:], nq.dtype)
            ng[side] = jnp.zeros(ng.shape[1:], ng.dtype)
            dq_in[side] = jnp.zeros(dq_in.shape[1:], dq_in.dtype)
            nstat[side] = jnp.full(nstat.shape[1:], FAR, nstat.dtype)

    if inside:
        text_copy(cross, cross, 0).wait_recv()
        for peer in peers:
            push(cross, peer)
        push(cross, mate)

    def own_step(h, carry):
        cols = head(h)
        dq, dk, dv = block_grads(
            q_ref[:, cols], g_ref[:, cols], k_ref[:, cols], v_ref[:, cols],
            stat[2, pl.ds(h, 1), :], stat[2, pl.ds(HEADS + h, 1), :],
        )
        dq_sum[:, cols] = dq
        dk_sum[:, cols] = dk
        dv_sum[:, cols] = dv
        return carry

    lax.fori_loop(0, HEADS, own_step, 0)

    line = lax.broadcasted_iota(jnp.int32, (TEXT, 1), 0)
    if inside:
        for peer in peers:
            for piece in (peer, peer + 2 - 4 * cross_bit):
                text_copy(piece, mate, 0).wait_recv()
                push(piece, mate)
        for device in [me] + peers:
            mates = device + 1 - 2 * core
            for piece in (mates, mates + 2 - 4 * cross_bit):
                text_copy(piece, mate, 0).wait_recv()
        spot = line // share
        place = (lax.rem(spot, half) * 2 + spot // half) * share + lax.rem(line, share)
    else:
        text[0] = tk_ref[...]
        text[1] = tv_ref[...]
        place = line
    valid = place < len_ref[0]

    def text_step(h, carry):
        cols = head(h)
        dq, dk, dv = block_grads(
            q_ref[:, cols], g_ref[:, cols], text[0, :, cols], text[1, :, cols],
            sums_ref[pl.ds(h, 1), :], stat[2, pl.ds(HEADS + h, 1), :], valid,
        )
        dq_sum[:, cols] += dq
        tgrad[0, :, cols] = dk
        tgrad[1, :, cols] = dv
        return carry

    lax.fori_loop(0, HEADS, text_step, 0)

    if inside:
        rest = half * share
        pair = 2 * share

        def span(start, size):
            return pl.ds(pl.multiple_of(start, share), size)

        part1[...] = tgrad[:, span((1 - core) * rest, rest), :].astype(jnp.bfloat16)
        copy1 = remote(part1, got1, r1.at[0], r1.at[1], mate)
        copy1.start()

    def window_step(c, carry):
        for side in range(2):

            @pl.when(has[side])
            def _():
                for copy in in_copies(1 - side, c):
                    copy.wait_recv()

        for i in range(GROUP):
            h = c * GROUP + i
            cols = head(h)
            dk_all, dv_all = dk_sum[:, cols], dv_sum[:, cols]
            for side in range(2):
                dq, dk, dv = block_grads(
                    nq[side, :, cols], ng[side, :, cols], k_ref[:, cols], v_ref[:, cols],
                    nstat[side, pl.ds(h, 1), :], nstat[side, pl.ds(HEADS + h, 1), :],
                )
                dq_out[side, :, cols] = dq.astype(jnp.bfloat16)
                dk_all, dv_all = dk_all + dk, dv_all + dv
            dk_ref[:, cols] = dk_all.astype(jnp.bfloat16)
            dv_ref[:, cols] = dv_all.astype(jnp.bfloat16)
        for side in range(2):

            @pl.when(has[side])
            def _():
                dq_copy(side, c).start()

        return carry

    for side in range(2):

        @pl.when(has[side])
        def _():
            stat_copy(1 - side).wait_recv()

    lax.fori_loop(0, CHUNKS // 3, window_step, 0)

    if inside:
        copy1.wait_recv()
        copies2 = []
        for d in range(1, outer):
            there = lax.rem(layer + d, outer)
            part2[d - 1] = (
                tgrad[:, span(core * rest + there * pair, pair), :]
                + got1[:, span(there * pair, pair), :].astype(jnp.float32)
            ).astype(jnp.bfloat16)
            copy = remote(
                part2.at[d - 1], got2.at[d - 1], r2.at[0, d - 1], r2.at[1, d - 1], peers[d - 1]
            )
            copy.start()
            copies2.append(copy)

    lax.fori_loop(CHUNKS // 3, CHUNKS - 1, window_step, 0)

    if inside:
        total = tgrad[:, span(core * rest + layer * pair, pair), :] + got1[
            :, span(layer * pair, pair), :
        ].astype(jnp.float32)
        for d, copy in enumerate(copies2):
            copy.wait_recv()
            total = total + got2[d].astype(jnp.float32)
        sum3[...] = total
        part3[...] = sum3[:, span((1 - cross_bit) * share, share), :].astype(jnp.bfloat16)
        copy3 = remote(part3, got3, r3.at[0], r3.at[1], cross)
        copy3.start()

    lax.fori_loop(CHUNKS - 1, CHUNKS, window_step, 0)

    if inside:
        copy3.wait_recv()
        mine = sum3[:, span(cross_bit * share, share), :] + got3[...].astype(jnp.float32)
        tdk_ref[...] = mine[0].astype(jnp.bfloat16)
        tdv_ref[...] = mine[1].astype(jnp.bfloat16)
    else:
        tdk_ref[...] = tgrad[0]
        tdv_ref[...] = tgrad[1]

    def last_step(c, carry):
        for side in range(2):

            @pl.when(has[side])
            def _():
                dq_copy(1 - side, c).wait_recv()

        cols = columns(c)
        dq_ref[:, cols] = (
            dq_sum[:, cols]
            + dq_in[0, :, cols].astype(jnp.float32)
            + dq_in[1, :, cols].astype(jnp.float32)
        ).astype(jnp.bfloat16)
        return carry

    lax.fori_loop(0, CHUNKS, last_step, 0)

    for side in range(2):

        @pl.when(has[side])
        def _():
            def step(c, carry):
                for copy in in_copies(side, c):
                    copy.wait_send()
                dq_copy(side, c).wait_send()
                return carry

            lax.fori_loop(0, CHUNKS, step, 0)
            stat_copy(side).wait_send()

    if inside:
        for copy in text_copies + [copy1] + copies2 + [copy3]:
            copy.wait_send()


def local(
    queries, video_keys, video_values, attn_out, out_grad, log_sums, text_keys, text_values,
    window, text_len,
):
    n = lax.axis_size("seq")
    tile, width = queries.shape
    share = TEXT // n
    inside = n % 4 == 0 and n >= 8 and share % 16 == 0
    low, wide = jnp.bfloat16, jnp.float32
    if not inside:
        text_keys = lax.all_gather(text_keys, "seq", axis=0, tiled=True)
        text_values = lax.all_gather(text_values, "seq", axis=0, tiled=True)
    text_out = jax.ShapeDtypeStruct(text_keys.shape, low if inside else wide)
    vmem, dma = pltpu.VMEM, pltpu.SemaphoreType.DMA
    scratch = [
        vmem((tile, width), low), vmem((tile, width), low),
        vmem((2, tile, width), low), vmem((2, tile, width), low),
        vmem((3, 2 * HEADS, tile), wide), vmem((2, 2 * HEADS, tile), wide),
        vmem((tile, width), wide), vmem((tile, width), wide), vmem((tile, width), wide),
        vmem((2, tile, width), low), vmem((2, tile, width), low),
        vmem((2, TEXT, width), low), vmem((2, TEXT, width), wide),
        dma((2,)), dma((2, 2, CHUNKS)), dma((2, 2, CHUNKS)),
        dma((2,)), dma((2,)), dma((2, CHUNKS)), dma((2, CHUNKS)),
    ]
    if inside:
        scratch += [
            dma((n - 1,)), dma((n,)),
            vmem((2, TEXT // 2, width), low), vmem((2, TEXT // 2, width), low),
            vmem((n // 4 - 1, 2, 2 * share, width), low), vmem((n // 4 - 1, 2, 2 * share, width), low),
            vmem((2, 2 * share, width), wide),
            vmem((2, share, width), low), vmem((2, share, width), low),
            dma((2,)), dma((2, n // 4 - 1)), dma((2,)),
        ]
    hbm, on_chip = pl.BlockSpec(memory_space=pl.ANY), pl.BlockSpec(memory_space=pltpu.VMEM)
    scalars = pl.BlockSpec(memory_space=pltpu.SMEM)
    video_out = jax.ShapeDtypeStruct((tile, width), low)
    dq, dk, dv, tdk, tdv = pl.pallas_call(
        functools.partial(kernel, n, inside),
        out_shape=(video_out, video_out, video_out, text_out, text_out),
        in_specs=[hbm, hbm] + [on_chip] * 6 + [scalars] * 2,
        out_specs=[on_chip] * 5,
        scratch_shapes=scratch,
        compiler_params=pltpu.CompilerParams(
            collective_id=0, has_side_effects=True, vmem_limit_bytes=48 * 2**20
        ),
    )(
        queries, out_grad, video_keys, video_values, attn_out, log_sums, text_keys, text_values,
        window, text_len,
    )
    if not inside:
        tdk = lax.psum_scatter(tdk, "seq", scatter_dimension=0, tiled=True).astype(low)
        tdv = lax.psum_scatter(tdv, "seq", scatter_dimension=0, tiled=True).astype(low)
    return dq, dk, dv, tdk, tdv


def solution(mesh):
    rows, every = P(("grp", "seq"), None), P()
    return jax.shard_map(
        local,
        mesh=mesh,
        in_specs=(rows, rows, rows, rows, rows, P(None, ("grp", "seq")), rows, rows, every, P("grp")),
        out_specs=(rows, rows, rows, rows, rows),
        check_vma=False,
    )
```

```python
import functools

import jax
import jax.numpy as jnp
from jax import lax
from jax.experimental import pallas as pl
from jax.experimental.pallas import tpu as pltpu
from jax.sharding import PartitionSpec as P

HEADS = 12
HEAD_DIM = 128
TEXT = 256
GROUP = 2
CHUNKS = HEADS // GROUP
FACTOR = HEAD_DIM ** (-0.5)
FAR = 1e30
MESH = pl.DeviceIdType.MESH


def mm(a, b, ca, cb):
    return lax.dot_general(a, b, (((ca,), (cb,)), ((), ())), preferred_element_type=jnp.float32)


def block_grads(q, g, k, v, sums, deltas, valid=None):
    probs = jnp.exp(mm(k, q, 1, 1) * FACTOR - sums)
    if valid is not None:
        probs = jnp.where(valid, probs, 0.0)
    dprobs = mm(v, g, 1, 1)
    dscores = (probs * (dprobs - deltas)).astype(jnp.bfloat16)
    dq = mm(dscores, k, 0, 0) * FACTOR
    dk = mm(dscores, q, 1, 0) * FACTOR
    dv = mm(probs.astype(jnp.bfloat16), g, 1, 0)
    return dq, dk, dv


def head(h):
    return pl.ds(pl.multiple_of(h * HEAD_DIM, HEAD_DIM), HEAD_DIM)


def kernel(
    n, inside, q_any, g_any, k_any, v_any, o_any, sums_ref, tk_any, tv_any, win_ref, len_ref,
    dq_ref, dk_ref, dv_ref, tdk_ref, tdv_ref,
    q_ref, g_ref, k_ref, v_ref, o_ref, nq, ng, stat, nstat, dq_sum, dk_sum, dv_sum, dq_out, dq_in, text, tgrad,
    local_sem, in_send, in_recv, stat_send, stat_recv, dq_send, dq_recv,
    *more,
):
    me = lax.axis_index("seq")
    has = (me > 0, me < n - 1)
    near = (me - 1, me + 1)
    share = TEXT // n
    half, outer = n // 2, n // 4
    core, cross_bit, layer = lax.rem(me, 2), lax.rem(me // 2, 2), me // 4
    mate, cross = me + 1 - 2 * core, me + 2 - 4 * cross_bit
    peers = [lax.rem(layer + d, outer) * 4 + lax.rem(me, 4) for d in range(1, outer)]

    own_text = pl.ds(pl.multiple_of((core * half + me // 2) * share, share), share)
    loads = [
        pltpu.make_async_copy(src, dst, local_sem.at[i])
        for i, (src, dst) in enumerate((
            (tk_any, text.at[0, own_text, :] if inside else text.at[0]),
            (tv_any, text.at[1, own_text, :] if inside else text.at[1]),
            (g_any, g_ref), (o_any, o_ref), (q_any, q_ref), (k_any, k_ref), (v_any, v_ref),
        ))
    ]
    for load in loads:
        load.start()

    def signal(device):
        pl.semaphore_signal(barrier, inc=1, device_id={"seq": device}, device_id_type=MESH)

    def remote(src, dst, send, recv, device):
        return pltpu.make_async_remote_copy(
            src_ref=src, dst_ref=dst, send_sem=send, recv_sem=recv,
            device_id={"seq": device}, device_id_type=MESH,
        )

    barrier = pltpu.get_barrier_semaphore()
    for side in range(2):
        pl.when(has[side])(functools.partial(signal, near[side]))
    far = [cross] + peers if inside else []
    for device in far:
        signal(device)
    pl.semaphore_wait(barrier, len(far) + sum(side.astype(jnp.int32) for side in has))

    def columns(c):
        return pl.ds(pl.multiple_of(c * GROUP * HEAD_DIM, GROUP * HEAD_DIM), GROUP * HEAD_DIM)

    def in_copies(side, c):
        there = 1 - side
        return [
            remote(
                src.at[:, columns(c)], dst.at[there, :, columns(c)],
                in_send.at[i, there, c], in_recv.at[i, there, c], near[side],
            )
            for i, (src, dst) in enumerate(((q_any, nq), (g_any, ng)))
        ]

    def stat_copy(side):
        there = 1 - side
        return remote(
            stat.at[side], nstat.at[there], stat_send.at[there], stat_recv.at[there], near[side]
        )

    def dq_copy(side, c):
        there = 1 - side
        return remote(
            dq_out.at[side, :, columns(c)], dq_in.at[there, :, columns(c)],
            dq_send.at[there, c], dq_recv.at[there, c], near[side],
        )

    if inside:
        t_send, t_recv, part1, got1, part2, got2, sum3, part3, got3, r1, r2, r3 = more

        def slot(device):
            return lax.rem(device, 2) * half + device // 2

        def rows(device):
            return pl.ds(pl.multiple_of(slot(device) * share, share), share)

        def text_copy(piece, device, kind):
            ref = text.at[:, rows(piece), :]
            return remote(ref, ref, t_send.at[kind, piece], t_recv.at[piece], device)

        def pair(at):
            own = at * 4 + lax.rem(me, 4)
            return own, own + 2 - 4 * cross_bit

        pushed = []

        def push(pieces, device, kind, condition=None):
            def every(act):
                def go():
                    for piece in pieces:
                        getattr(text_copy(piece, device, kind), act)()

                if condition is None:
                    go()
                else:
                    pl.when(condition)(go)

            every("start")
            pushed.append(every)

        def chain_send(step):
            low, high = layer - (step - 1), layer + (step - 1)
            push(pair(low), me + 4, 2, (layer < outer - 1) & (low >= 0))
            push(pair(high), me - 4, 3, (layer > 0) & (high < outer))

        def chain_recv(step):
            for at, there in ((layer - step, layer >= step), (layer + step, layer + step < outer)):

                @pl.when(there)
                def _():
                    for piece in pair(at):
                        text_copy(piece, mate, 1).wait_recv()

                push(pair(at), mate, 1, there)

        for load in loads[:2]:
            load.wait()
        push([me], cross, 0)
        push([me], mate, 1)

    for side in range(2):

        @pl.when(has[side])
        def _():
            def step(c, carry):
                for copy in in_copies(side, c):
                    copy.start()
                return carry

            lax.fori_loop(0, CHUNKS, step, 0)

    for load in loads[2 if inside else 0 : 4]:
        load.wait()

    def delta_step(h, carry):
        cols = head(h)
        prod = g_ref[:, cols].astype(jnp.float32) * o_ref[:, cols].astype(jnp.float32)
        row = jnp.sum(prod.T, axis=0, keepdims=True)
        for side in range(3):
            stat[side, pl.ds(HEADS + h, 1), :] = row
        return carry

    lax.fori_loop(0, HEADS, delta_step, 0)
    lane = lax.broadcasted_iota(jnp.int32, win_ref.shape, 1)
    weights = jnp.sum(jnp.where(lane == me, win_ref[...], 0), axis=1, keepdims=True)
    for index, offset in enumerate((0, 2, 1)):
        bias = jnp.where(weights[offset : offset + 1] > 0, 0.0, FAR)
        stat[index, :HEADS, :] = sums_ref[...] + bias
    for side in range(2):

        @pl.when(has[side])
        def _():
            stat_copy(side).start()

        @pl.when(jnp.logical_not(has[side]))
        def _():
            nq[side] = jnp.zeros(nq.shape[1:], nq.dtype)
            ng[side] = jnp.zeros(ng.shape[1:], ng.dtype)
            dq_in[side] = jnp.zeros(dq_in.shape[1:], dq_in.dtype)
            nstat[side] = jnp.full(nstat.shape[1:], FAR, nstat.dtype)

    if inside:
        text_copy(cross, cross, 0).wait_recv()
        push([cross], mate, 1)
        chain_send(1)

    for load in loads[4:]:
        load.wait()

    def own_step(h, carry):
        cols = head(h)
        dq, dk, dv = block_grads(
            q_ref[:, cols], g_ref[:, cols], k_ref[:, cols], v_ref[:, cols],
            stat[2, pl.ds(h, 1), :], stat[2, pl.ds(HEADS + h, 1), :],
        )
        dq_sum[:, cols] = dq
        dk_sum[:, cols] = dk
        dv_sum[:, cols] = dv
        return carry

    if inside:
        done = 0
        for step in range(1, outer):
            upto = HEADS * step // (outer - 1)
            lax.fori_loop(done, upto, own_step, 0)
            done = upto
            chain_recv(step)
            if step < outer - 1:
                chain_send(step + 1)
    else:
        lax.fori_loop(0, HEADS, own_step, 0)

    line = lax.broadcasted_iota(jnp.int32, (TEXT, 1), 0)
    if inside:
        for at in range(outer):
            piece = at * 4 + lax.rem(mate, 4)
            for one in (piece, piece + 2 - 4 * cross_bit):
                text_copy(one, mate, 1).wait_recv()
        spot = line // share
        place = (lax.rem(spot, half) * 2 + spot // half) * share + lax.rem(line, share)
    else:
        place = line
    valid = place < len_ref[0]

    def text_step(h, carry):
        cols = head(h)
        dq, dk, dv = block_grads(
            q_ref[:, cols], g_ref[:, cols], text[0, :, cols], text[1, :, cols],
            sums_ref[pl.ds(h, 1), :], stat[2, pl.ds(HEADS + h, 1), :], valid,
        )
        dq_sum[:, cols] += dq
        tgrad[0, :, cols] = dk
        tgrad[1, :, cols] = dv
        return carry

    lax.fori_loop(0, HEADS, text_step, 0)

    if inside:
        rest = half * share
        pair = 2 * share

        def span(start, size):
            return pl.ds(pl.multiple_of(start, share), size)

        part1[...] = tgrad[:, span((1 - core) * rest, rest), :].astype(jnp.bfloat16)
        copy1 = remote(part1, got1, r1.at[0], r1.at[1], mate)
        copy1.start()

    def window_step(c, carry):
        for side in range(2):

            @pl.when(has[side])
            def _():
                for copy in in_copies(1 - side, c):
                    copy.wait_recv()

        for i in range(GROUP):
            h = c * GROUP + i
            cols = head(h)
            dk_all, dv_all = dk_sum[:, cols], dv_sum[:, cols]
            for side in range(2):
                dq, dk, dv = block_grads(
                    nq[side, :, cols], ng[side, :, cols], k_ref[:, cols], v_ref[:, cols],
                    nstat[side, pl.ds(h, 1), :], nstat[side, pl.ds(HEADS + h, 1), :],
                )
                dq_out[side, :, cols] = dq.astype(jnp.bfloat16)
                dk_all, dv_all = dk_all + dk, dv_all + dv
            dk_ref[:, cols] = dk_all.astype(jnp.bfloat16)
            dv_ref[:, cols] = dv_all.astype(jnp.bfloat16)
        for side in range(2):

            @pl.when(has[side])
            def _():
                dq_copy(side, c).start()

        return carry

    for side in range(2):

        @pl.when(has[side])
        def _():
            stat_copy(1 - side).wait_recv()

    lax.fori_loop(0, CHUNKS // 3, window_step, 0)

    if inside:
        copy1.wait_recv()
        copies2 = []
        for d in range(1, outer):
            there = lax.rem(layer + d, outer)
            part2[d - 1] = (
                tgrad[:, span(core * rest + there * pair, pair), :]
                + got1[:, span(there * pair, pair), :].astype(jnp.float32)
            ).astype(jnp.bfloat16)
            copy = remote(
                part2.at[d - 1], got2.at[d - 1], r2.at[0, d - 1], r2.at[1, d - 1], peers[d - 1]
            )
            copy.start()
            copies2.append(copy)

    lax.fori_loop(CHUNKS // 3, CHUNKS - 1, window_step, 0)

    if inside:
        total = tgrad[:, span(core * rest + layer * pair, pair), :] + got1[
            :, span(layer * pair, pair), :
        ].astype(jnp.float32)
        for d, copy in enumerate(copies2):
            copy.wait_recv()
            total = total + got2[d].astype(jnp.float32)
        sum3[...] = total
        part3[...] = sum3[:, span((1 - cross_bit) * share, share), :].astype(jnp.bfloat16)
        copy3 = remote(part3, got3, r3.at[0], r3.at[1], cross)
        copy3.start()

    lax.fori_loop(CHUNKS - 1, CHUNKS, window_step, 0)

    if inside:
        copy3.wait_recv()
        mine = sum3[:, span(cross_bit * share, share), :] + got3[...].astype(jnp.float32)
        tdk_ref[...] = mine[0].astype(jnp.bfloat16)
        tdv_ref[...] = mine[1].astype(jnp.bfloat16)
    else:
        tdk_ref[...] = tgrad[0]
        tdv_ref[...] = tgrad[1]

    def last_step(c, carry):
        for side in range(2):

            @pl.when(has[side])
            def _():
                dq_copy(1 - side, c).wait_recv()

        cols = columns(c)
        dq_ref[:, cols] = (
            dq_sum[:, cols]
            + dq_in[0, :, cols].astype(jnp.float32)
            + dq_in[1, :, cols].astype(jnp.float32)
        ).astype(jnp.bfloat16)
        return carry

    lax.fori_loop(0, CHUNKS, last_step, 0)

    for side in range(2):

        @pl.when(has[side])
        def _():
            def step(c, carry):
                for copy in in_copies(side, c):
                    copy.wait_send()
                dq_copy(side, c).wait_send()
                return carry

            lax.fori_loop(0, CHUNKS, step, 0)
            stat_copy(side).wait_send()

    if inside:
        for every in pushed:
            every("wait_send")
        for copy in [copy1] + copies2 + [copy3]:
            copy.wait_send()


def local(
    queries, video_keys, video_values, attn_out, out_grad, log_sums, text_keys, text_values,
    window, text_len,
):
    n = lax.axis_size("seq")
    tile, width = queries.shape
    share = TEXT // n
    inside = n % 4 == 0 and n >= 8 and share % 16 == 0
    low, wide = jnp.bfloat16, jnp.float32
    if not inside:
        text_keys = lax.all_gather(text_keys, "seq", axis=0, tiled=True)
        text_values = lax.all_gather(text_values, "seq", axis=0, tiled=True)
    text_out = jax.ShapeDtypeStruct(text_keys.shape, low if inside else wide)
    vmem, dma = pltpu.VMEM, pltpu.SemaphoreType.DMA
    scratch = [
        *[vmem((tile, width), low)] * 5,
        vmem((2, tile, width), low), vmem((2, tile, width), low),
        vmem((3, 2 * HEADS, tile), wide), vmem((2, 2 * HEADS, tile), wide),
        vmem((tile, width), wide), vmem((tile, width), wide), vmem((tile, width), wide),
        vmem((2, tile, width), low), vmem((2, tile, width), low),
        vmem((2, TEXT, width), low), vmem((2, TEXT, width), wide),
        dma((7,)), dma((2, 2, CHUNKS)), dma((2, 2, CHUNKS)),
        dma((2,)), dma((2,)), dma((2, CHUNKS)), dma((2, CHUNKS)),
    ]
    if inside:
        scratch += [
            dma((4, n)), dma((n,)),
            vmem((2, TEXT // 2, width), low), vmem((2, TEXT // 2, width), low),
            vmem((n // 4 - 1, 2, 2 * share, width), low), vmem((n // 4 - 1, 2, 2 * share, width), low),
            vmem((2, 2 * share, width), wide),
            vmem((2, share, width), low), vmem((2, share, width), low),
            dma((2,)), dma((2, n // 4 - 1)), dma((2,)),
        ]
    hbm, on_chip = pl.BlockSpec(memory_space=pl.ANY), pl.BlockSpec(memory_space=pltpu.VMEM)
    scalars = pl.BlockSpec(memory_space=pltpu.SMEM)
    video_out = jax.ShapeDtypeStruct((tile, width), low)
    dq, dk, dv, tdk, tdv = pl.pallas_call(
        functools.partial(kernel, n, inside),
        out_shape=(video_out, video_out, video_out, text_out, text_out),
        in_specs=[hbm] * 5 + [on_chip, hbm, hbm, on_chip, scalars],
        out_specs=[on_chip] * 5,
        scratch_shapes=scratch,
        compiler_params=pltpu.CompilerParams(
            collective_id=0, has_side_effects=True, vmem_limit_bytes=62 * 2**20
        ),
    )(
        queries, out_grad, video_keys, video_values, attn_out, log_sums, text_keys, text_values,
        window.T, text_len,
    )
    if not inside:
        tdk = lax.psum_scatter(tdk, "seq", scatter_dimension=0, tiled=True).astype(low)
        tdv = lax.psum_scatter(tdv, "seq", scatter_dimension=0, tiled=True).astype(low)
    return dq, dk, dv, tdk, tdv


def solution(mesh):
    rows, every = P(("grp", "seq"), None), P()
    return jax.shard_map(
        local,
        mesh=mesh,
        in_specs=(rows, rows, rows, rows, rows, P(None, ("grp", "seq")), rows, rows, every, P("grp")),
        out_specs=(rows, rows, rows, rows, rows),
        check_vma=False,
    )
```

```python
import functools

import jax
import jax.numpy as jnp
from jax import lax
from jax.experimental import pallas as pl
from jax.experimental.pallas import tpu as pltpu
from jax.sharding import PartitionSpec as P

HEADS = 12
HEAD_DIM = 128
TEXT = 256
GROUP = 2
CHUNKS = HEADS // GROUP
FACTOR = HEAD_DIM ** (-0.5)
FAR = 1e30
PACE = (0, 1, 2, 3, 4, 5, 6)
SPLIT = (1, 3, 5)
MESH = pl.DeviceIdType.MESH


def mm(a, b, ca, cb):
    return lax.dot_general(a, b, (((ca,), (cb,)), ((), ())), preferred_element_type=jnp.float32)


def block_grads(q, g, k, v, sums, deltas, valid=None):
    probs = jnp.exp(mm(k, q, 1, 1) * FACTOR - sums)
    if valid is not None:
        probs = jnp.where(valid, probs, 0.0)
    dprobs = mm(v, g, 1, 1)
    dscores = (probs * (dprobs - deltas)).astype(jnp.bfloat16)
    dq = mm(dscores, k, 0, 0) * FACTOR
    dk = mm(dscores, q, 1, 0) * FACTOR
    dv = mm(probs.astype(jnp.bfloat16), g, 1, 0)
    return dq, dk, dv


def head(h):
    return pl.ds(pl.multiple_of(h * HEAD_DIM, HEAD_DIM), HEAD_DIM)


def kernel(
    n, inside, q_any, g_any, k_any, v_any, o_any, sums_ref, tk_any, tv_any, win_ref, len_ref,
    dq_ref, dk_ref, dv_ref, tdk_ref, tdv_ref,
    q_ref, g_ref, k_ref, v_ref, o_ref, nq, ng, stat, nstat, dq_sum, dk_sum, dv_sum, dq_out, dq_in, text, tgrad,
    local_sem, in_send, in_recv, stat_send, stat_recv, dq_send, dq_recv,
    *more,
):
    me = lax.axis_index("seq")
    share = TEXT // n
    half, outer = n // 2, n // 4
    core, cross_bit, layer = lax.rem(me, 2), lax.rem(me // 2, 2), me // 4
    mate, cross = me + 1 - 2 * core, me + 2 - 4 * cross_bit
    close, wide = 1 - core, core
    far = me - 1 + 2 * wide
    has_far = (far >= 0) & (far < n)
    corner = core == cross_bit
    odd, high = lax.rem(layer, 2), lax.rem(layer // 2, 2)
    next_layer, leap_layer = layer + 1 - 2 * odd, layer + 2 - 4 * high
    step_on, leap = next_layer * 4 + lax.rem(me, 4), leap_layer * 4 + lax.rem(me, 4)
    peers = [step_on, leap]

    own_text = pl.ds(pl.multiple_of((core * half + me // 2) * share, share), share)
    loads = [
        pltpu.make_async_copy(src, dst, local_sem.at[i])
        for i, (src, dst) in enumerate((
            (tk_any, text.at[0, own_text, :] if inside else text.at[0]),
            (tv_any, text.at[1, own_text, :] if inside else text.at[1]),
            (g_any, g_ref), (o_any, o_ref), (q_any, q_ref), (k_any, k_ref), (v_any, v_ref),
        ))
    ]
    for load in loads:
        load.start()

    def signal(device):
        pl.semaphore_signal(barrier, inc=1, device_id={"seq": device}, device_id_type=MESH)

    def remote(src, dst, send, recv, device):
        return pltpu.make_async_remote_copy(
            src_ref=src, dst_ref=dst, send_sem=send, recv_sem=recv,
            device_id={"seq": device}, device_id_type=MESH,
        )

    barrier = pltpu.get_barrier_semaphore()
    known = [mate] + ([cross] + peers if inside else [])
    for device in known:
        signal(device)
    pl.when(has_far)(functools.partial(signal, far))
    pl.semaphore_wait(barrier, len(known) + has_far.astype(jnp.int32))

    def near(side):
        return me - 1 + 2 * side

    def far_only(go):
        pl.when(has_far)(go)

    def always(go):
        go()

    def columns(c):
        return pl.ds(pl.multiple_of(c * GROUP * HEAD_DIM, GROUP * HEAD_DIM), GROUP * HEAD_DIM)

    def in_copies(side, c):
        there = 1 - side
        return [
            remote(
                src.at[:, columns(c)], dst.at[there, :, columns(c)],
                in_send.at[i, there, c], in_recv.at[i, there, c], near(side),
            )
            for i, (src, dst) in enumerate(((q_any, nq), (g_any, ng)))
        ]

    def stat_copy(side):
        there = 1 - side
        return remote(
            stat.at[side], nstat.at[there], stat_send.at[there], stat_recv.at[there], near(side)
        )

    def dq_copy(side, c):
        there = 1 - side
        return remote(
            dq_out.at[side, :, columns(c)], dq_in.at[there, :, columns(c)],
            dq_send.at[there, c], dq_recv.at[there, c], near(side),
        )

    if inside:
        t_send, t_recv, part1, got1, part2, got2, sum3, part3, got3, r1, r2, r3 = more

        def slot(device):
            return lax.rem(device, 2) * half + device // 2

        def rows(device):
            return pl.ds(pl.multiple_of(slot(device) * share, share), share)

        def text_copy(piece, device, kind):
            ref = text.at[:, rows(piece), :]
            return remote(ref, ref, t_send.at[kind, piece], t_recv.at[piece], device)

        def pair(at):
            own = at * 4 + lax.rem(me, 4)
            return own, own + 2 - 4 * cross_bit

        def arrive(*pieces):
            for piece in pieces:
                text_copy(piece, mate, 1).wait_recv()

        pushed = []

        def push(device, kind, *pieces):
            for piece in pieces:
                copy = text_copy(piece, device, kind)
                copy.start()
                pushed.append(copy)

        for load in loads[:2]:
            load.wait()
        push(cross, 0, me)
        push(leap, 2, me)
        push(step_on, 3, me)
        push(mate, 1, me)

    def send_in(side, first=0, end=CHUNKS):
        def step(c, carry):
            for copy in in_copies(side, c):
                copy.start()
            return carry

        lax.fori_loop(first, end, step, 0)

    def send_far(stage):
        first, end = PACE[stage], PACE[stage + 1]
        if first < end:
            far_only(functools.partial(send_in, wide, first, end))

    send_in(close)
    send_far(0)

    for load in loads[2 if inside else 0 : 4]:
        load.wait()

    def delta_step(h, carry):
        cols = head(h)
        prod = g_ref[:, cols].astype(jnp.float32) * o_ref[:, cols].astype(jnp.float32)
        row = jnp.sum(prod.T, axis=0, keepdims=True)
        for side in range(3):
            stat[side, pl.ds(HEADS + h, 1), :] = row
        return carry

    lax.fori_loop(0, HEADS, delta_step, 0)
    lane = lax.broadcasted_iota(jnp.int32, win_ref.shape, 1)
    weights = jnp.sum(jnp.where(lane == me, win_ref[...], 0), axis=1, keepdims=True)
    for index, offset in enumerate((0, 2, 1)):
        bias = jnp.where(weights[offset : offset + 1] > 0, 0.0, FAR)
        stat[index, :HEADS, :] = sums_ref[...] + bias
    stat_copy(close).start()
    far_only(lambda: stat_copy(wide).start())

    @pl.when(jnp.logical_not(has_far))
    def _():
        nq[wide] = jnp.zeros(nq.shape[1:], nq.dtype)
        ng[wide] = jnp.zeros(ng.shape[1:], ng.dtype)
        dq_in[wide] = jnp.zeros(dq_in.shape[1:], dq_in.dtype)
        nstat[wide] = jnp.full(nstat.shape[1:], FAR, nstat.dtype)

    if inside:
        arrive(cross)
        push(leap, 2, cross)
        push(step_on, 3, cross)
        push(mate, 1, cross)

    for load in loads[4:]:
        load.wait()

    def own_step(h, carry):
        cols = head(h)
        dq, dk, dv = block_grads(
            q_ref[:, cols], g_ref[:, cols], k_ref[:, cols], v_ref[:, cols],
            stat[2, pl.ds(h, 1), :], stat[2, pl.ds(HEADS + h, 1), :],
        )
        dq_sum[:, cols] = dq
        dk_sum[:, cols] = dk
        dv_sum[:, cols] = dv
        return carry

    lax.fori_loop(0, HEADS // 2, own_step, 0)
    send_far(1)
    lax.fori_loop(HEADS // 2, HEADS, own_step, 0)
    send_far(2)
    if inside:
        arrive(*pair(leap_layer))
        push(step_on, 3, *pair(leap_layer))
        push(mate, 1, *pair(leap_layer))

    def window_step(side, where, last, c, carry):
        @where
        def _():
            for copy in in_copies(1 - side, c):
                copy.wait_recv()

        for i in range(GROUP):
            h = c * GROUP + i
            cols = head(h)
            dq, dk, dv = block_grads(
                nq[side, :, cols], ng[side, :, cols], k_ref[:, cols], v_ref[:, cols],
                nstat[side, pl.ds(h, 1), :], nstat[side, pl.ds(HEADS + h, 1), :],
            )
            dq_out[side, :, cols] = dq.astype(jnp.bfloat16)
            if last:
                dk_ref[:, cols] = (dk_sum[:, cols] + dk).astype(jnp.bfloat16)
                dv_ref[:, cols] = (dv_sum[:, cols] + dv).astype(jnp.bfloat16)
            else:
                dk_sum[:, cols] += dk
                dv_sum[:, cols] += dv

        @where
        def _():
            dq_copy(side, c).start()

        return carry

    mate_step = functools.partial(window_step, close, always, False)
    far_step = functools.partial(window_step, wide, far_only, True)
    stat_copy(1 - close).wait_recv()
    lax.fori_loop(0, CHUNKS // 2, mate_step, 0)
    if inside:
        for at in (next_layer, next_layer + 2 - 4 * high):
            arrive(*pair(at))
            push(mate, 1, *pair(at))
    send_far(3)
    lax.fori_loop(CHUNKS // 2, CHUNKS, mate_step, 0)
    send_far(4)
    far_only(lambda: stat_copy(1 - wide).wait_recv())

    line = lax.broadcasted_iota(jnp.int32, (TEXT, 1), 0)
    if inside:
        for at in range(outer):
            piece = at * 4 + lax.rem(mate, 4)
            arrive(piece, piece + 2 - 4 * cross_bit)
        spot = line // share
        place = (lax.rem(spot, half) * 2 + spot // half) * share + lax.rem(line, share)
    else:
        place = line
    valid = place < len_ref[0]

    def text_step(h, carry):
        cols = head(h)
        dq, dk, dv = block_grads(
            q_ref[:, cols], g_ref[:, cols], text[0, :, cols], text[1, :, cols],
            sums_ref[pl.ds(h, 1), :], stat[2, pl.ds(HEADS + h, 1), :], valid,
        )
        dq_sum[:, cols] += dq
        tgrad[0, :, cols] = dk
        tgrad[1, :, cols] = dv
        return carry

    lax.fori_loop(0, HEADS // 2, text_step, 0)
    send_far(5)
    lax.fori_loop(HEADS // 2, HEADS, text_step, 0)

    if inside:
        rest = half * share
        pair_rows = 2 * share

        def span(start, size):
            return pl.ds(pl.multiple_of(start, share), size)

        part1[...] = tgrad[:, span((1 - core) * rest, rest), :].astype(jnp.bfloat16)
        copy1 = remote(part1, got1, r1.at[0], r1.at[1], mate)
        copy1.start()

    lax.fori_loop(0, SPLIT[0], far_step, 0)

    if inside:
        copy1.wait_recv()
        def kept(at):
            return tgrad[:, span(core * rest + at * pair_rows, pair_rows), :] + got1[
                :, span(at * pair_rows, pair_rows), :
            ].astype(jnp.float32)

        for i in range(2):
            part2[i] = kept(1 - odd + 2 * i).astype(jnp.bfloat16)
        copy2 = remote(part2.at[:2], got2.at[:2], r2.at[0, 0], r2.at[1, 0], step_on)
        copy2.start()

    lax.fori_loop(SPLIT[0], SPLIT[1], far_step, 0)

    if inside:
        copy2.wait_recv()
        part2[2] = (kept(leap_layer) + got2[1 - high].astype(jnp.float32)).astype(jnp.bfloat16)
        copy4 = remote(part2.at[2], got2.at[2], r2.at[0, 1], r2.at[1, 1], leap)
        copy4.start()

    lax.fori_loop(SPLIT[1], SPLIT[2], far_step, 0)

    if inside:
        copy4.wait_recv()
        total = kept(layer) + got2[high].astype(jnp.float32) + got2[2].astype(jnp.float32)
        sum3[...] = total
        part3[...] = sum3[:, span((1 - cross_bit) * share, share), :].astype(jnp.bfloat16)
        copy3 = remote(part3, got3, r3.at[0], r3.at[1], cross)
        copy3.start()

    lax.fori_loop(SPLIT[2], CHUNKS, far_step, 0)

    if inside:
        copy3.wait_recv()
        mine = sum3[:, span(cross_bit * share, share), :] + got3[...].astype(jnp.float32)
        tdk_ref[...] = mine[0].astype(jnp.bfloat16)
        tdv_ref[...] = mine[1].astype(jnp.bfloat16)
    else:
        tdk_ref[...] = tgrad[0]
        tdv_ref[...] = tgrad[1]

    def last_step(c, carry):
        dq_copy(1 - close, c).wait_recv()
        far_only(lambda: dq_copy(1 - wide, c).wait_recv())
        cols = columns(c)
        dq_ref[:, cols] = (
            dq_sum[:, cols]
            + dq_in[0, :, cols].astype(jnp.float32)
            + dq_in[1, :, cols].astype(jnp.float32)
        ).astype(jnp.bfloat16)
        return carry

    lax.fori_loop(0, CHUNKS, last_step, 0)

    def finish(side):
        def step(c, carry):
            for copy in in_copies(side, c):
                copy.wait_send()
            dq_copy(side, c).wait_send()
            return carry

        lax.fori_loop(0, CHUNKS, step, 0)
        stat_copy(side).wait_send()

    finish(close)
    far_only(functools.partial(finish, wide))

    if inside:
        for copy in pushed + [copy1, copy2, copy4, copy3]:
            copy.wait_send()


def local(
    queries, video_keys, video_values, attn_out, out_grad, log_sums, text_keys, text_values,
    window, text_len,
):
    n = lax.axis_size("seq")
    tile, width = queries.shape
    share = TEXT // n
    inside = n == 16 and share % 16 == 0
    low, wide = jnp.bfloat16, jnp.float32
    if not inside:
        text_keys = lax.all_gather(text_keys, "seq", axis=0, tiled=True)
        text_values = lax.all_gather(text_values, "seq", axis=0, tiled=True)
    text_out = jax.ShapeDtypeStruct(text_keys.shape, low if inside else wide)
    vmem, dma = pltpu.VMEM, pltpu.SemaphoreType.DMA
    scratch = [
        *[vmem((tile, width), low)] * 5,
        vmem((2, tile, width), low), vmem((2, tile, width), low),
        vmem((3, 2 * HEADS, tile), wide), vmem((2, 2 * HEADS, tile), wide),
        vmem((tile, width), wide), vmem((tile, width), wide), vmem((tile, width), wide),
        vmem((2, tile, width), low), vmem((2, tile, width), low),
        vmem((2, TEXT, width), low), vmem((2, TEXT, width), wide),
        dma((7,)), dma((2, 2, CHUNKS)), dma((2, 2, CHUNKS)),
        dma((2,)), dma((2,)), dma((2, CHUNKS)), dma((2, CHUNKS)),
    ]
    if inside:
        scratch += [
            dma((4, n)), dma((n,)),
            vmem((2, TEXT // 2, width), low), vmem((2, TEXT // 2, width), low),
            vmem((3, 2, 2 * share, width), low), vmem((3, 2, 2 * share, width), low),
            vmem((2, 2 * share, width), wide),
            vmem((2, share, width), low), vmem((2, share, width), low),
            dma((2,)), dma((2, 2)), dma((2,)),
        ]
    hbm, on_chip = pl.BlockSpec(memory_space=pl.ANY), pl.BlockSpec(memory_space=pltpu.VMEM)
    scalars = pl.BlockSpec(memory_space=pltpu.SMEM)
    video_out = jax.ShapeDtypeStruct((tile, width), low)
    dq, dk, dv, tdk, tdv = pl.pallas_call(
        functools.partial(kernel, n, inside),
        out_shape=(video_out, video_out, video_out, text_out, text_out),
        in_specs=[hbm] * 5 + [on_chip, hbm, hbm, on_chip, scalars],
        out_specs=[on_chip] * 5,
        scratch_shapes=scratch,
        compiler_params=pltpu.CompilerParams(
            collective_id=0, has_side_effects=True, vmem_limit_bytes=62 * 2**20
        ),
    )(
        queries, out_grad, video_keys, video_values, attn_out, log_sums, text_keys, text_values,
        window.T, text_len,
    )
    if not inside:
        tdk = lax.psum_scatter(tdk, "seq", scatter_dimension=0, tiled=True).astype(low)
        tdv = lax.psum_scatter(tdv, "seq", scatter_dimension=0, tiled=True).astype(low)
    return dq, dk, dv, tdk, tdv


def solution(mesh):
    rows, every = P(("grp", "seq"), None), P()
    return jax.shard_map(
        local,
        mesh=mesh,
        in_specs=(rows, rows, rows, rows, rows, P(None, ("grp", "seq")), rows, rows, every, P("grp")),
        out_specs=(rows, rows, rows, rows, rows),
        check_vma=False,
    )
```

```python
import functools

import jax
import jax.numpy as jnp
from jax import lax
from jax.experimental import pallas as pl
from jax.experimental.pallas import tpu as pltpu
from jax.sharding import PartitionSpec as P

HEADS = 12
HEAD_DIM = 128
TEXT = 256
GROUP = 2
CHUNKS = HEADS // GROUP
FACTOR = HEAD_DIM ** (-0.5)
FAR = 1e30
PACE = (0, 1, 2, 3, 4, 5, 6)
EARLY = (1, 2)
SPLIT = (2, 4, 5)
MESH = pl.DeviceIdType.MESH


def mm(a, b, ca, cb):
    return lax.dot_general(a, b, (((ca,), (cb,)), ((), ())), preferred_element_type=jnp.float32)


def block_grads(q, g, k, v, sums, deltas, valid=None):
    probs = jnp.exp(mm(k, q, 1, 1) * FACTOR - sums)
    if valid is not None:
        probs = jnp.where(valid, probs, 0.0)
    dprobs = mm(v, g, 1, 1)
    dscores = (probs * (dprobs - deltas)).astype(jnp.bfloat16)
    dq = mm(dscores, k, 0, 0) * FACTOR
    dk = mm(dscores, q, 1, 0) * FACTOR
    dv = mm(probs.astype(jnp.bfloat16), g, 1, 0)
    return dq, dk, dv


def head(h):
    return pl.ds(pl.multiple_of(h * HEAD_DIM, HEAD_DIM), HEAD_DIM)


def kernel(
    n, inside, q_any, g_any, k_any, v_any, o_any, sums_ref, tk_any, tv_any, win_ref, len_ref,
    dq_ref, dk_ref, dv_ref, tdk_ref, tdv_ref,
    q_ref, g_ref, k_ref, v_ref, o_ref, nq, ng, stat, nstat, dq_sum, dk_sum, dv_sum, dq_out, dq_in, text, tgrad,
    local_sem, in_send, in_recv, stat_send, stat_recv, dq_send, dq_recv,
    *more,
):
    me = lax.axis_index("seq")
    share = TEXT // n
    half, outer = n // 2, n // 4
    core, cross_bit, layer = lax.rem(me, 2), lax.rem(me // 2, 2), me // 4
    mate, cross = me + 1 - 2 * core, me + 2 - 4 * cross_bit
    close, wide = 1 - core, core
    far = me - 1 + 2 * wide
    has_far = (far >= 0) & (far < n)
    corner = core == cross_bit
    odd, high = lax.rem(layer, 2), lax.rem(layer // 2, 2)
    next_layer, leap_layer = layer + 1 - 2 * odd, layer + 2 - 4 * high
    step_on, leap = next_layer * 4 + lax.rem(me, 4), leap_layer * 4 + lax.rem(me, 4)
    peers = [step_on, leap]

    own_text = pl.ds(pl.multiple_of((core * half + me // 2) * share, share), share)
    loads = [
        pltpu.make_async_copy(src, dst, local_sem.at[i])
        for i, (src, dst) in enumerate((
            (tk_any, text.at[0, own_text, :] if inside else text.at[0]),
            (tv_any, text.at[1, own_text, :] if inside else text.at[1]),
            (g_any, g_ref), (o_any, o_ref), (q_any, q_ref), (k_any, k_ref), (v_any, v_ref),
        ))
    ]
    for load in loads:
        load.start()

    def signal(device):
        pl.semaphore_signal(barrier, inc=1, device_id={"seq": device}, device_id_type=MESH)

    def remote(src, dst, send, recv, device):
        return pltpu.make_async_remote_copy(
            src_ref=src, dst_ref=dst, send_sem=send, recv_sem=recv,
            device_id={"seq": device}, device_id_type=MESH,
        )

    barrier = pltpu.get_barrier_semaphore()
    known = [mate] + ([cross] + peers if inside else [])
    for device in known:
        signal(device)
    pl.when(has_far)(functools.partial(signal, far))
    pl.semaphore_wait(barrier, len(known) + has_far.astype(jnp.int32))

    def near(side):
        return me - 1 + 2 * side

    def far_only(go):
        pl.when(has_far)(go)

    def always(go):
        go()

    def columns(c):
        return pl.ds(pl.multiple_of(c * GROUP * HEAD_DIM, GROUP * HEAD_DIM), GROUP * HEAD_DIM)

    def in_copies(side, c):
        there = 1 - side
        return [
            remote(
                src.at[:, columns(c)], dst.at[there, :, columns(c)],
                in_send.at[i, there, c], in_recv.at[i, there, c], near(side),
            )
            for i, (src, dst) in enumerate(((q_any, nq), (g_any, ng)))
        ]

    def stat_copy(side):
        there = 1 - side
        return remote(
            stat.at[side], nstat.at[there], stat_send.at[there], stat_recv.at[there], near(side)
        )

    def dq_copy(side, c):
        there = 1 - side
        return remote(
            dq_out.at[side, :, columns(c)], dq_in.at[there, :, columns(c)],
            dq_send.at[there, c], dq_recv.at[there, c], near(side),
        )

    if inside:
        t_send, t_recv, part1, got1, part2, got2, sum3, part3, got3, r1, r2, r3 = more

        def slot(device):
            return lax.rem(device, 2) * half + device // 2

        def rows(device):
            return pl.ds(pl.multiple_of(slot(device) * share, share), share)

        def text_copy(piece, device, kind):
            ref = text.at[:, rows(piece), :]
            return remote(ref, ref, t_send.at[kind, piece], t_recv.at[piece], device)

        def pair(at):
            own = at * 4 + lax.rem(me, 4)
            return own, own + 2 - 4 * cross_bit

        def arrive(*pieces):
            for piece in pieces:
                text_copy(piece, mate, 1).wait_recv()

        pushed = []

        def push(device, kind, *pieces):
            for piece in pieces:
                copy = text_copy(piece, device, kind)
                copy.start()
                pushed.append(copy)

        for load in loads[:2]:
            load.wait()
        push(cross, 0, me)
        push(leap, 2, me)
        push(step_on, 3, me)
        push(mate, 1, me)

    def send_in(side, first=0, end=CHUNKS):
        def step(c, carry):
            for copy in in_copies(side, c):
                copy.start()
            return carry

        lax.fori_loop(first, end, step, 0)

    def send_far(stage):
        first, end = PACE[stage], PACE[stage + 1]
        if first < end:
            far_only(functools.partial(send_in, wide, first, end))

    send_in(close)
    send_far(0)

    for load in loads[2 if inside else 0 : 4]:
        load.wait()

    def delta_step(h, carry):
        cols = head(h)
        prod = g_ref[:, cols].astype(jnp.float32) * o_ref[:, cols].astype(jnp.float32)
        row = jnp.sum(prod.T, axis=0, keepdims=True)
        for side in range(3):
            stat[side, pl.ds(HEADS + h, 1), :] = row
        return carry

    lax.fori_loop(0, HEADS, delta_step, 0)
    lane = lax.broadcasted_iota(jnp.int32, win_ref.shape, 1)
    weights = jnp.sum(jnp.where(lane == me, win_ref[...], 0), axis=1, keepdims=True)
    for index, offset in enumerate((0, 2, 1)):
        bias = jnp.where(weights[offset : offset + 1] > 0, 0.0, FAR)
        stat[index, :HEADS, :] = sums_ref[...] + bias
    stat_copy(close).start()
    far_only(lambda: stat_copy(wide).start())

    @pl.when(jnp.logical_not(has_far))
    def _():
        nq[wide] = jnp.zeros(nq.shape[1:], nq.dtype)
        ng[wide] = jnp.zeros(ng.shape[1:], ng.dtype)
        dq_in[wide] = jnp.zeros(dq_in.shape[1:], dq_in.dtype)
        nstat[wide] = jnp.full(nstat.shape[1:], FAR, nstat.dtype)

    if inside:
        arrive(cross)
        push(leap, 2, cross)
        push(step_on, 3, cross)
        push(mate, 1, cross)

    for load in loads[4:]:
        load.wait()

    def own_step(h, carry):
        cols = head(h)
        dq, dk, dv = block_grads(
            q_ref[:, cols], g_ref[:, cols], k_ref[:, cols], v_ref[:, cols],
            stat[2, pl.ds(h, 1), :], stat[2, pl.ds(HEADS + h, 1), :],
        )
        dq_sum[:, cols] = dq
        dk_sum[:, cols] = dk
        dv_sum[:, cols] = dv
        return carry

    lax.fori_loop(0, HEADS // 2, own_step, 0)
    send_far(1)
    lax.fori_loop(HEADS // 2, HEADS, own_step, 0)
    send_far(2)
    if inside:
        arrive(*pair(leap_layer))
        push(step_on, 3, *pair(leap_layer))
        push(mate, 1, *pair(leap_layer))

    def window_step(side, where, last, c, carry):
        @where
        def _():
            for copy in in_copies(1 - side, c):
                copy.wait_recv()

        for i in range(GROUP):
            h = c * GROUP + i
            cols = head(h)
            dq, dk, dv = block_grads(
                nq[side, :, cols], ng[side, :, cols], k_ref[:, cols], v_ref[:, cols],
                nstat[side, pl.ds(h, 1), :], nstat[side, pl.ds(HEADS + h, 1), :],
            )
            dq_out[side, :, cols] = dq.astype(jnp.bfloat16)
            if last:
                dk_ref[:, cols] = (dk_sum[:, cols] + dk).astype(jnp.bfloat16)
                dv_ref[:, cols] = (dv_sum[:, cols] + dv).astype(jnp.bfloat16)
            else:
                dk_sum[:, cols] += dk
                dv_sum[:, cols] += dv

        @where
        def _():
            dq_copy(side, c).start()

        return carry

    mate_step = functools.partial(window_step, close, always, False)
    far_step = functools.partial(window_step, wide, far_only, True)
    stat_copy(1 - close).wait_recv()
    lax.fori_loop(0, CHUNKS // 2, mate_step, 0)
    far_only(lambda: stat_copy(1 - wide).wait_recv())
    lax.fori_loop(0, EARLY[0], far_step, 0)
    if inside:
        for at in (next_layer, next_layer + 2 - 4 * high):
            arrive(*pair(at))
            push(mate, 1, *pair(at))
    send_far(3)
    lax.fori_loop(CHUNKS // 2, CHUNKS, mate_step, 0)
    send_far(4)
    lax.fori_loop(EARLY[0], EARLY[1], far_step, 0)

    line = lax.broadcasted_iota(jnp.int32, (TEXT, 1), 0)
    if inside:
        for at in range(outer):
            piece = at * 4 + lax.rem(mate, 4)
            arrive(piece, piece + 2 - 4 * cross_bit)
        spot = line // share
        place = (lax.rem(spot, half) * 2 + spot // half) * share + lax.rem(line, share)
    else:
        place = line
    valid = place < len_ref[0]

    def text_step(h, carry):
        cols = head(h)
        dq, dk, dv = block_grads(
            q_ref[:, cols], g_ref[:, cols], text[0, :, cols], text[1, :, cols],
            sums_ref[pl.ds(h, 1), :], stat[2, pl.ds(HEADS + h, 1), :], valid,
        )
        dq_sum[:, cols] += dq
        tgrad[0, :, cols] = dk
        tgrad[1, :, cols] = dv
        return carry

    lax.fori_loop(0, HEADS // 2, text_step, 0)
    send_far(5)
    lax.fori_loop(HEADS // 2, HEADS, text_step, 0)

    if inside:
        rest = half * share
        pair_rows = 2 * share

        def span(start, size):
            return pl.ds(pl.multiple_of(start, share), size)

        part1[...] = tgrad[:, span((1 - core) * rest, rest), :].astype(jnp.bfloat16)
        copy1 = remote(part1, got1, r1.at[0], r1.at[1], mate)
        copy1.start()

    lax.fori_loop(EARLY[1], SPLIT[0], far_step, 0)

    if inside:
        copy1.wait_recv()
        def kept(at):
            return tgrad[:, span(core * rest + at * pair_rows, pair_rows), :] + got1[
                :, span(at * pair_rows, pair_rows), :
            ].astype(jnp.float32)

        for i in range(2):
            part2[i] = kept(1 - odd + 2 * i).astype(jnp.bfloat16)
        copy2 = remote(part2.at[:2], got2.at[:2], r2.at[0, 0], r2.at[1, 0], step_on)
        copy2.start()

    lax.fori_loop(SPLIT[0], SPLIT[1], far_step, 0)

    if inside:
        copy2.wait_recv()
        part2[2] = (kept(leap_layer) + got2[1 - high].astype(jnp.float32)).astype(jnp.bfloat16)
        copy4 = remote(part2.at[2], got2.at[2], r2.at[0, 1], r2.at[1, 1], leap)
        copy4.start()

    lax.fori_loop(SPLIT[1], SPLIT[2], far_step, 0)

    if inside:
        copy4.wait_recv()
        total = kept(layer) + got2[high].astype(jnp.float32) + got2[2].astype(jnp.float32)
        sum3[...] = total
        part3[...] = sum3[:, span((1 - cross_bit) * share, share), :].astype(jnp.bfloat16)
        copy3 = remote(part3, got3, r3.at[0], r3.at[1], cross)
        copy3.start()

    lax.fori_loop(SPLIT[2], CHUNKS, far_step, 0)

    if inside:
        copy3.wait_recv()
        mine = sum3[:, span(cross_bit * share, share), :] + got3[...].astype(jnp.float32)
        tdk_ref[...] = mine[0].astype(jnp.bfloat16)
        tdv_ref[...] = mine[1].astype(jnp.bfloat16)
    else:
        tdk_ref[...] = tgrad[0]
        tdv_ref[...] = tgrad[1]

    def last_step(c, carry):
        dq_copy(1 - close, c).wait_recv()
        far_only(lambda: dq_copy(1 - wide, c).wait_recv())
        cols = columns(c)
        dq_ref[:, cols] = (
            dq_sum[:, cols]
            + dq_in[0, :, cols].astype(jnp.float32)
            + dq_in[1, :, cols].astype(jnp.float32)
        ).astype(jnp.bfloat16)
        return carry

    lax.fori_loop(0, CHUNKS, last_step, 0)

    def finish(side):
        def step(c, carry):
            for copy in in_copies(side, c):
                copy.wait_send()
            dq_copy(side, c).wait_send()
            return carry

        lax.fori_loop(0, CHUNKS, step, 0)
        stat_copy(side).wait_send()

    finish(close)
    far_only(functools.partial(finish, wide))

    if inside:
        for copy in pushed + [copy1, copy2, copy4, copy3]:
            copy.wait_send()


def hand_over(*refs):
    inputs, outputs, held, sem = refs[:5], refs[5:10], refs[10:15], refs[15]
    loads = [pltpu.make_async_copy(inputs[i], held[i], sem.at[0, i]) for i in range(5)]
    stores = [pltpu.make_async_copy(held[i], outputs[i], sem.at[1, i]) for i in range(5)]
    for load in loads:
        load.start()
    for load, store in zip(loads, stores):
        load.wait()
        store.start()
    for store in stores:
        store.wait()


def local(
    queries, video_keys, video_values, attn_out, out_grad, log_sums, text_keys, text_values,
    window, text_len,
):
    n = lax.axis_size("seq")
    tile, width = queries.shape
    share = TEXT // n
    inside = n == 16 and share % 16 == 0
    low, wide = jnp.bfloat16, jnp.float32
    if not inside:
        text_keys = lax.all_gather(text_keys, "seq", axis=0, tiled=True)
        text_values = lax.all_gather(text_values, "seq", axis=0, tiled=True)
    text_out = jax.ShapeDtypeStruct(text_keys.shape, low if inside else wide)
    vmem, dma = pltpu.VMEM, pltpu.SemaphoreType.DMA
    scratch = [
        *[vmem((tile, width), low)] * 5,
        vmem((2, tile, width), low), vmem((2, tile, width), low),
        vmem((3, 2 * HEADS, tile), wide), vmem((2, 2 * HEADS, tile), wide),
        vmem((tile, width), wide), vmem((tile, width), wide), vmem((tile, width), wide),
        vmem((2, tile, width), low), vmem((2, tile, width), low),
        vmem((2, TEXT, width), low), vmem((2, TEXT, width), wide),
        dma((7,)), dma((2, 2, CHUNKS)), dma((2, 2, CHUNKS)),
        dma((2,)), dma((2,)), dma((2, CHUNKS)), dma((2, CHUNKS)),
    ]
    if inside:
        scratch += [
            dma((4, n)), dma((n,)),
            vmem((2, TEXT // 2, width), low), vmem((2, TEXT // 2, width), low),
            vmem((3, 2, 2 * share, width), low), vmem((3, 2, 2 * share, width), low),
            vmem((2, 2 * share, width), wide),
            vmem((2, share, width), low), vmem((2, share, width), low),
            dma((2,)), dma((2, 2)), dma((2,)),
        ]
    hbm, on_chip = pl.BlockSpec(memory_space=pl.ANY), pl.BlockSpec(memory_space=pltpu.VMEM)
    scalars = pl.BlockSpec(memory_space=pltpu.SMEM)
    video_out = jax.ShapeDtypeStruct((tile, width), low)
    results = pl.pallas_call(
        functools.partial(kernel, n, inside),
        out_shape=(video_out, video_out, video_out, text_out, text_out),
        in_specs=[hbm] * 5 + [on_chip, hbm, hbm, on_chip, scalars],
        out_specs=[on_chip] * 5,
        scratch_shapes=scratch,
        compiler_params=pltpu.CompilerParams(
            collective_id=0, has_side_effects=True, vmem_limit_bytes=62 * 2**20
        ),
    )(
        queries, out_grad, video_keys, video_values, attn_out, log_sums, text_keys, text_values,
        window.T, text_len,
    )
    shapes = [video_out] * 3 + [text_out] * 2
    dq, dk, dv, tdk, tdv = pl.pallas_call(
        hand_over,
        out_shape=shapes,
        in_specs=[hbm] * 5,
        out_specs=[hbm] * 5,
        scratch_shapes=[vmem(one.shape, one.dtype) for one in shapes] + [dma((2, 5))],
        compiler_params=pltpu.CompilerParams(vmem_limit_bytes=62 * 2**20),
    )(*results)
    if not inside:
        tdk = lax.psum_scatter(tdk, "seq", scatter_dimension=0, tiled=True).astype(low)
        tdv = lax.psum_scatter(tdv, "seq", scatter_dimension=0, tiled=True).astype(low)
    return dq, dk, dv, tdk, tdv


def solution(mesh):
    rows, every = P(("grp", "seq"), None), P()
    return jax.shard_map(
        local,
        mesh=mesh,
        in_specs=(rows, rows, rows, rows, rows, P(None, ("grp", "seq")), rows, rows, every, P("grp")),
        out_specs=(rows, rows, rows, rows, rows),
        check_vma=False,
    )
```
